32 devices in a mesh: hyp: 4 (over z), row: 2 (over x), col: 4 (over y, core).
Axes of the slice: x: 2, y: 2, z: 4, core: 2. Of those that a mesh axis runs over, the one named last changes fastest.
Arguments:
- front_orig: bfloat16 [40960, 10240], P(('hyp', 'row'), 'col'), parts along dimension 0, as said below
- child_updates: bfloat16 [65536, 8192], P(('hyp', 'row'), 'col'), parts along dimension 0, as said below
- child_map: int32 [8, 64], P('hyp'), parts along dimension 0, may hold values from 0 to 79, as said below
- panel_inverse: bfloat16 [1024, 256], P('hyp'), parts along dimension 0, as said below
Outputs:
- schur: bfloat16 [40960, 10240], P(('hyp', 'row'), 'col'), parts along dimension 0
- panel: bfloat16 [40960, 256], P(('hyp', 'row')), parts along dimension 0
The draws below stay inside these ranges and needn't reach their ends.
There are 4 independent parts, one for each index of `hyp`. The reference program is written for one: setup_inputs(seed, part) draws one part's arguments, and reference() takes and returns one part's arrays. A program takes and returns all parts, laid end to end along the dimension named above; each array names one. Nothing has to cross between parts.
Inputs may be any that keep to these rules, and one draw needn't show every extreme that they name: `child_map`: each child's entries are distinct. Parent block p lies on row index p // 40 and column index p // 20. Of the 64 blocks of a child on one row index (child c on row indices c * 1 to (c + 1) - 1, in order), at most 32 lie on one parent row index; of the 16 blocks on one column index, at most 4 lie on one parent column index. Every parent row index receives the same number of blocks of each child. `child_updates`: each child's update block is symmetric. `front_orig`: Symmetric. `panel_inverse`: upper triangular with a positive diagonal.
All inputs are finite; a program needn't handle non-finite values.
Results may differ from the reference program's by a relative error of at most 0.0052.
Values may be sent and summed in bfloat16 or wider, within the bound.
A program may use at most 256 MiB of HBM per device.

```python
import math
import jax
import jax.numpy as jnp

F = 10240
C = 8192
B = 128
PANEL = 256
CB = 64
NF = 4
MB = 20
RUN = 16


def draw_front_orig(key, part):
    raw = jax.random.normal(key, (F, F), jnp.float32)
    return ((raw + raw.T) * 0.5).astype(jnp.bfloat16)


def draw_child_updates(key, part):
    raw = jax.random.normal(key, (2, C, C), jnp.float32)
    sym = (raw + jnp.swapaxes(raw, 1, 2)) * 0.5
    return sym.reshape(2 * C, C).astype(jnp.bfloat16)


def draw_child_map(key, part):
    picks = CB // NF
    maps = []
    for child_index in range(2):
        base = jax.random.fold_in(key, 11 + child_index)
        key_owner, key_runs, key_slots = jax.random.split(base, 3)
        owner_perm = jax.random.permutation(key_owner, NF).astype(jnp.int32)
        run_keys = jax.random.split(key_runs, CB // RUN)
        run_perm = jax.vmap(lambda k: jax.random.permutation(k, RUN))(run_keys).astype(jnp.int32)
        order = (jnp.arange(CB // RUN, dtype=jnp.int32)[:, None] * RUN + run_perm).reshape(CB)
        fine = owner_perm[order % NF]
        slot_index = order // NF

        def subset(k):
            key_mid, key_mix = jax.random.split(k)
            middle = (jax.random.permutation(key_mid, MB - 2) + 1).astype(jnp.int32)
            chosen = jnp.concatenate([jnp.array([0, MB - 1], jnp.int32), middle[:picks - 2]])
            return jax.random.permutation(key_mix, chosen).astype(jnp.int32)
        table = jax.vmap(subset)(jax.random.split(key_slots, NF))
        inner = table[fine, slot_index]
        maps.append(fine * MB + inner)
    return jnp.stack(maps).astype(jnp.int32)


def draw_panel_inverse(key, part):
    key_diag, key_off = jax.random.split(key)
    rows_at = jnp.arange(PANEL, dtype=jnp.int32)[:, None]
    cols_at = jnp.arange(PANEL, dtype=jnp.int32)[None, :]
    diag_vals = jnp.exp(jax.random.uniform(key_diag, (PANEL,), jnp.float32, math.log(0.04), math.log(0.15)))
    off_vals = jax.random.normal(key_off, (PANEL, PANEL), jnp.float32) * 0.008
    result = jnp.where(rows_at == cols_at, diag_vals[:, None], jnp.where(cols_at > rows_at, off_vals, 0.0))
    return result.astype(jnp.bfloat16)


def setup_inputs(seed: int = 0, part: int = 0) -> dict:
    seeds = jax.random.split(jax.random.key(seed), 5)
    own_keys = jax.random.split(jax.random.fold_in(seeds[4], part), 5)
    return {
        "front_orig": draw_front_orig(jax.random.fold_in(jax.random.fold_in(seeds[4], part), 71), part),
        "child_updates": draw_child_updates(jax.random.fold_in(jax.random.fold_in(seeds[4], part), 71), part),
        "child_map": draw_child_map(jax.random.fold_in(jax.random.fold_in(seeds[4], part), 71), part),
        "panel_inverse": draw_panel_inverse(jax.random.fold_in(jax.random.fold_in(seeds[4], part), 71), part),
    }


def reference(front_orig, child_updates, child_map, panel_inverse):
    offsets = jnp.arange(B, dtype=jnp.int32)
    front32 = front_orig.astype(jnp.float32)
    for child_index in range(2):
        update_block = child_updates[child_index * C:(child_index + 1) * C].astype(jnp.float32)
        indices = (child_map[child_index].astype(jnp.int32)[:, None] * B + offsets[None, :]).reshape(C).astype(jnp.int32)
        front32 = front32.at[indices[:, None], indices[None, :]].add(update_block)
    front = front32.astype(jnp.bfloat16)
    panel = jnp.dot(front[:, :PANEL], panel_inverse, preferred_element_type=jnp.float32).astype(jnp.bfloat16)
    update = jnp.dot(panel, panel.T, preferred_element_type=jnp.float32)
    schur = (front.astype(jnp.float32) - update).astype(jnp.bfloat16)
    return schur, panel
```

```python
import functools

import jax
import jax.numpy as jnp
from jax import lax
from jax.experimental import pallas as pl
from jax.experimental.pallas import tpu as pltpu
from jax.sharding import PartitionSpec as P

B = 128
PANEL = 256
PANEL_BLOCKS = PANEL // B
VMEM_LIMIT = 48 * 1024 * 1024


def largest_group(count, limit):
    return max(g for g in range(1, limit + 1) if count % g == 0)


def rank_in_owner(ids, owners):
    same = owners[..., :, None] == owners[..., None, :]
    smaller = ids[..., None, :] < ids[..., :, None]
    return jnp.sum(same & smaller, axis=-1, dtype=jnp.int32)


def source_of_slot(ids, owner_width, capacity, owners_count):
    owners = ids // owner_width
    slots = owners * capacity + rank_in_owner(ids, owners)
    match = slots[None, :] == jnp.arange(owners_count * capacity, dtype=jnp.int32)[:, None]
    return jnp.sum(jnp.where(match, jnp.arange(ids.shape[0], dtype=jnp.int32)[None, :], 0), axis=1)


def pack_kernel(group, n_col, col_cap, first, width, row_src, col_src, *refs):
    out = refs[group]
    for c in range(n_col):
        for b in range(width):
            src = pl.multiple_of(col_src[c * col_cap + first + b] * B, B)
            for g in range(group):
                out[0, c, g * B:(g + 1) * B, b * B:(b + 1) * B] = refs[g][:, pl.ds(src, B)]


def pack(child, row_src, col_src, n_row, n_col, row_cap, col_cap, first, width):
    group = largest_group(row_cap, 4)
    steps = row_cap // group
    cols = child.shape[1]

    def row_map(g, r, s, row_src, col_src):
        return (row_src[r * row_cap + s * group + g], 0)

    out_shape = (n_row, n_col, row_cap * B, width * B)
    size = n_row * n_col * row_cap * width * B * B
    return pl.pallas_call(
        functools.partial(pack_kernel, group, n_col, col_cap, first, width),
        grid_spec=pltpu.PrefetchScalarGridSpec(
            num_scalar_prefetch=2,
            grid=(n_row, steps),
            in_specs=[pl.BlockSpec((B, cols), functools.partial(row_map, g)) for g in range(group)],
            out_specs=pl.BlockSpec(
                (1, n_col, group * B, width * B), lambda r, s, row_src, col_src: (r, 0, s, 0)
            ),
        ),
        out_shape=jax.ShapeDtypeStruct(out_shape, jnp.bfloat16),
        compiler_params=pltpu.CompilerParams(vmem_limit_bytes=VMEM_LIMIT),
        cost_estimate=pl.CostEstimate(
            flops=0, bytes_accessed=2 * child.size + 2 * size, transcendentals=0
        ),
    )(row_src, col_src, *([child] * group))


def add_tiles(acc, group, chunks, n_col, col_cap, has_row, col_to, tiles):
    step = pl.program_id(0)
    for g in range(group):
        for k in range(2):
            @pl.when(has_row[k, step * group + g] > 0)
            def _():
                for h, (first, width) in enumerate(chunks):
                    ref = tiles[(g * 2 + k) * len(chunks) + h]
                    for t in range(n_col):
                        for b in range(width):
                            at = pl.multiple_of(col_to[k, t * col_cap + first + b] * B, B)
                            acc[g * B:(g + 1) * B, pl.ds(at, B)] += ref[
                                0, t, :, b * B:(b + 1) * B
                            ].astype(jnp.float32)


def panel_kernel(group, chunks, n_col, col_cap, src, slot, has_row, col_to, *refs):
    front_ref, inverse_ref = refs[:2]
    tiles, out, acc = refs[2:-2], refs[-2], refs[-1]
    acc[:, :PANEL] = front_ref[...].astype(jnp.float32)
    add_tiles(acc, group, chunks, n_col, col_cap, has_row, col_to, tiles)
    out[...] = jnp.dot(
        acc[:, :PANEL].astype(jnp.bfloat16), inverse_ref[...], preferred_element_type=jnp.float32
    ).astype(jnp.bfloat16)


def schur_kernel(group, chunks, n_col, col_cap, strip, src, slot, has_row, col_to, *refs):
    front_ref, row_ref, col_ref = refs[:3]
    tiles, out, acc = refs[3:-2], refs[-2], refs[-1]
    width = front_ref.shape[1]
    acc[:, :width] = front_ref[...].astype(jnp.float32)
    add_tiles(acc, group, chunks, n_col, col_cap, has_row, col_to, tiles)
    for at in range(0, width, strip):
        update = lax.dot_general(
            row_ref[...], col_ref[at:at + strip, :], (((1,), (1,)), ((), ())),
            preferred_element_type=jnp.float32,
        )
        front = acc[:, at:at + strip].astype(jnp.bfloat16).astype(jnp.float32)
        out[:, at:at + strip] = (front - update).astype(jnp.bfloat16)


def gather_call(body, tables, front, extra, extra_specs, incoming, chunks, acc_cols, group, out_cols,
                front_cols, flops):
    rows = front.shape[0]
    specs, arrays = [], []

    def tile_map(g, k, s, src, slot, has_row, col_to):
        return (src[k, s * group + g], 0, slot[k, s * group + g], 0)

    for g in range(group):
        for k in range(2):
            for array in incoming:
                n_col, width = array.shape[1], array.shape[3]
                specs.append(pl.BlockSpec((1, n_col, B, width), functools.partial(tile_map, g, k)))
                arrays.append(array)
    moved = rows * (front_cols + out_cols) * 2 + sum(2 * a.size for a in incoming)
    return pl.pallas_call(
        body,
        grid_spec=pltpu.PrefetchScalarGridSpec(
            num_scalar_prefetch=4,
            grid=(rows // (group * B),),
            in_specs=[pl.BlockSpec((group * B, front_cols), lambda s, *_: (s, 0))]
            + extra_specs + specs,
            out_specs=pl.BlockSpec((group * B, out_cols), lambda s, *_: (s, 0)),
            scratch_shapes=[pltpu.VMEM((group * B, acc_cols), jnp.float32)],
        ),
        out_shape=jax.ShapeDtypeStruct((rows, out_cols), jnp.bfloat16),
        compiler_params=pltpu.CompilerParams(vmem_limit_bytes=VMEM_LIMIT),
        cost_estimate=pl.CostEstimate(flops=flops, bytes_accessed=moved, transcendentals=0),
    )(*tables, front, *extra, *arrays)


def local(front_orig, child_updates, child_map, panel_inverse):
    n_row = lax.axis_size("row")
    n_col = lax.axis_size("col")
    me_row = lax.axis_index("row")
    me_col = lax.axis_index("col")
    rows_local, cols_local = child_updates.shape
    part_rows, part_cols = front_orig.shape
    senders = n_row // 2
    blocks_row = rows_local // B
    blocks_col = cols_local // B
    fine_count = max(n_row, n_col)
    prb = part_rows // B
    pcb = part_cols // B
    row_cap = max(1, blocks_row // fine_count) * (fine_count // n_row)
    col_cap = max(1, blocks_col // fine_count) * (fine_count // n_col)

    my_map = lax.dynamic_index_in_dim(child_map, me_row // senders, 0, keepdims=False)
    row_ids = lax.dynamic_slice_in_dim(child_map.reshape(-1), me_row * blocks_row, blocks_row)
    col_ids = lax.dynamic_slice_in_dim(my_map, me_col * blocks_col, blocks_col)
    row_src = source_of_slot(row_ids, prb, row_cap, n_row)
    col_src = source_of_slot(col_ids, pcb, col_cap, n_col)

    by_row = child_map.reshape(n_row, blocks_row)
    row_rank = rank_in_owner(by_row, by_row // prb).reshape(2, -1)
    sender = jnp.broadcast_to(
        jnp.arange(n_row, dtype=jnp.int32)[:, None], by_row.shape
    ).reshape(2, -1)
    mine = me_row * prb + jnp.arange(prb, dtype=jnp.int32)
    match = by_row.reshape(2, 1, -1) == mine[None, :, None]
    src = jnp.sum(jnp.where(match, sender[:, None, :], 0), axis=2)
    slot = jnp.sum(jnp.where(match, row_rank[:, None, :], 0), axis=2)
    has_row = jnp.sum(match, axis=2, dtype=jnp.int32)

    by_col = child_map.reshape(2, n_col, blocks_col)
    col_owner = by_col // pcb
    col_rank = rank_in_owner(by_col, col_owner)
    match = (col_owner == me_col)[:, :, None, :] & (
        col_rank[:, :, None, :] == jnp.arange(col_cap, dtype=jnp.int32)[None, None, :, None]
    )
    col_to = pcb + jnp.sum(
        jnp.where(match, (by_col - me_col * pcb - pcb)[:, :, None, :], 0), axis=3
    ).reshape(2, n_col * col_cap)

    head = min(PANEL_BLOCKS, col_cap)
    chunks = [(0, head)] + ([(head, col_cap - head)] if col_cap > head else [])
    incoming = []
    for first, width in chunks:
        outgoing = pack(
            child_updates, row_src, col_src, n_row, n_col, row_cap, col_cap, first, width
        ).reshape(n_row * n_col, row_cap * B, width * B)
        arrived = lax.all_to_all(outgoing, ("row", "col"), split_axis=0, concat_axis=0, tiled=True)
        incoming.append(arrived.reshape(n_row, n_col, row_cap * B, width * B))

    group = largest_group(prb, 2)
    panel_to = jnp.minimum(col_to, PANEL_BLOCKS)
    local_panel = gather_call(
        functools.partial(panel_kernel, group, chunks[:1], n_col, col_cap),
        (src, slot, has_row, panel_to), front_orig, (panel_inverse,),
        [pl.BlockSpec((PANEL, PANEL), lambda s, *_: (0, 0))],
        incoming[:1], chunks[:1], PANEL + B, group, PANEL, PANEL,
        2 * part_rows * PANEL * PANEL,
    )
    masked = jnp.where(me_col == 0, local_panel, jnp.zeros_like(local_panel))
    row_panel = lax.psum(masked, "col")
    all_panel = lax.all_gather(row_panel, "row", axis=0, tiled=True)
    col_panel = lax.dynamic_slice_in_dim(all_panel, me_col * part_cols, part_cols, 0)
    strip = part_cols // largest_group(part_cols // PANEL, 5)
    schur = gather_call(
        functools.partial(schur_kernel, group, chunks, n_col, col_cap, strip),
        (src, slot, has_row, col_to), front_orig, (row_panel, col_panel),
        [
            pl.BlockSpec((group * B, PANEL), lambda s, *_: (s, 0)),
            pl.BlockSpec((part_cols, PANEL), lambda s, *_: (0, 0)),
        ],
        incoming, chunks, part_cols + B, group, part_cols, part_cols,
        2 * part_rows * part_cols * PANEL,
    )
    return (schur, row_panel)


def solution(mesh):
    in_specs = (P(("hyp", "row"), "col"), P(("hyp", "row"), "col"), P("hyp", None), P("hyp", None))
    out_specs = (P(("hyp", "row"), "col"), P(("hyp", "row"), None))
    return jax.shard_map(local, mesh=mesh, in_specs=in_specs, out_specs=out_specs, check_vma=False)
```

```python
import functools

import jax
import jax.numpy as jnp
from jax import lax
from jax.experimental import pallas as pl
from jax.experimental.pallas import tpu as pltpu
from jax.sharding import PartitionSpec as P

B = 128
PANEL = 256
PANEL_BLOCKS = PANEL // B
VMEM_LIMIT = 48 * 1024 * 1024


def largest_group(count, limit):
    return max(g for g in range(1, limit + 1) if count % g == 0)


def rank_in_owner(ids, owners):
    same = owners[..., :, None] == owners[..., None, :]
    smaller = ids[..., None, :] < ids[..., :, None]
    return jnp.sum(same & smaller, axis=-1, dtype=jnp.int32)


def source_of_slot(ids, owner_width, capacity, owners_count):
    owners = ids // owner_width
    slots = owners * capacity + rank_in_owner(ids, owners)
    match = slots[None, :] == jnp.arange(owners_count * capacity, dtype=jnp.int32)[:, None]
    return jnp.sum(jnp.where(match, jnp.arange(ids.shape[0], dtype=jnp.int32)[None, :], 0), axis=1)


def pack_kernel(group, n_col, col_cap, first, width, row_src, col_src, *refs):
    out = refs[group]
    for c in range(n_col):
        for b in range(width):
            src = pl.multiple_of(col_src[c * col_cap + first + b] * B, B)
            for g in range(group):
                out[0, c, g * B:(g + 1) * B, b * B:(b + 1) * B] = refs[g][:, pl.ds(src, B)]


def pack(child, row_src, col_src, n_row, n_col, row_cap, col_cap, first, width):
    group = largest_group(row_cap, 4)
    steps = row_cap // group
    cols = child.shape[1]

    def row_map(g, r, s, row_src, col_src):
        return (row_src[r * row_cap + s * group + g], 0)

    out_shape = (n_row, n_col, row_cap * B, width * B)
    size = n_row * n_col * row_cap * width * B * B
    return pl.pallas_call(
        functools.partial(pack_kernel, group, n_col, col_cap, first, width),
        grid_spec=pltpu.PrefetchScalarGridSpec(
            num_scalar_prefetch=2,
            grid=(n_row, steps),
            in_specs=[pl.BlockSpec((B, cols), functools.partial(row_map, g)) for g in range(group)],
            out_specs=pl.BlockSpec(
                (1, n_col, group * B, width * B), lambda r, s, row_src, col_src: (r, 0, s, 0)
            ),
        ),
        out_shape=jax.ShapeDtypeStruct(out_shape, jnp.bfloat16),
        compiler_params=pltpu.CompilerParams(vmem_limit_bytes=VMEM_LIMIT),
        cost_estimate=pl.CostEstimate(
            flops=0, bytes_accessed=2 * child.size + 2 * size, transcendentals=0
        ),
    )(row_src, col_src, *([child] * group))


def add_tiles(acc, group, chunks, n_col, col_cap, has_row, col_to, tiles):
    step = pl.program_id(0)
    for g in range(group):
        for k in range(2):
            @pl.when(has_row[k, step * group + g] > 0)
            def _():
                for h, (first, width) in enumerate(chunks):
                    ref = tiles[(g * 2 + k) * len(chunks) + h]
                    for t in range(n_col):
                        for b in range(width):
                            at = pl.multiple_of(col_to[k, t * col_cap + first + b] * B, B)
                            acc[g * B:(g + 1) * B, pl.ds(at, B)] += ref[
                                0, t, :, b * B:(b + 1) * B
                            ].astype(jnp.float32)


def panel_kernel(group, chunks, n_col, col_cap, src, slot, has_row, col_to, *refs):
    front_ref, inverse_ref = refs[:2]
    tiles, out, acc = refs[2:-2], refs[-2], refs[-1]
    acc[:, :PANEL] = front_ref[...].astype(jnp.float32)
    add_tiles(acc, group, chunks, n_col, col_cap, has_row, col_to, tiles)
    out[...] = jnp.dot(
        acc[:, :PANEL].astype(jnp.bfloat16), inverse_ref[...], preferred_element_type=jnp.float32
    ).astype(jnp.bfloat16)


def schur_kernel(group, chunks, n_col, col_cap, strip, src, slot, has_row, col_to, *refs):
    front_ref, row_ref, col_ref = refs[:3]
    tiles, out, acc = refs[3:-2], refs[-2], refs[-1]
    width = front_ref.shape[1]
    acc[:, :width] = front_ref[...].astype(jnp.float32)
    add_tiles(acc, group, chunks, n_col, col_cap, has_row, col_to, tiles)
    for at in range(0, width, strip):
        update = lax.dot_general(
            row_ref[...], col_ref[at:at + strip, :], (((1,), (1,)), ((), ())),
            preferred_element_type=jnp.float32,
        )
        front = acc[:, at:at + strip].astype(jnp.bfloat16).astype(jnp.float32)
        out[:, at:at + strip] = (front - update).astype(jnp.bfloat16)


def gather_call(body, tables, front, extra, extra_specs, incoming, chunks, acc_cols, group, out_cols,
                front_cols, flops):
    rows = front.shape[0]
    specs, arrays = [], []

    def tile_map(g, k, s, src, slot, has_row, col_to):
        return (src[k, s * group + g], 0, slot[k, s * group + g], 0)

    for g in range(group):
        for k in range(2):
            for array in incoming:
                n_col, width = array.shape[1], array.shape[3]
                specs.append(pl.BlockSpec((1, n_col, B, width), functools.partial(tile_map, g, k)))
                arrays.append(array)
    moved = rows * (front_cols + out_cols) * 2 + sum(2 * a.size for a in incoming)
    return pl.pallas_call(
        body,
        grid_spec=pltpu.PrefetchScalarGridSpec(
            num_scalar_prefetch=4,
            grid=(rows // (group * B),),
            in_specs=[pl.BlockSpec((group * B, front_cols), lambda s, *_: (s, 0))]
            + extra_specs + specs,
            out_specs=pl.BlockSpec((group * B, out_cols), lambda s, *_: (s, 0)),
            scratch_shapes=[pltpu.VMEM((group * B, acc_cols), jnp.float32)],
        ),
        out_shape=jax.ShapeDtypeStruct((rows, out_cols), jnp.bfloat16),
        compiler_params=pltpu.CompilerParams(vmem_limit_bytes=VMEM_LIMIT),
        cost_estimate=pl.CostEstimate(flops=flops, bytes_accessed=moved, transcendentals=0),
    )(*tables, front, *extra, *arrays)


def spread(value, pairs, receives):
    got = lax.ppermute(value, ("row", "col"), pairs)
    return jnp.where(receives, got, value)


def share_panel(panel, part_cols):
    n_row, n_col = lax.axis_size("row"), lax.axis_size("col")
    me_row, me_col = lax.axis_index("row"), lax.axis_index("col")
    part_rows = panel.shape[0]
    one_owner = part_rows % part_cols == 0
    groups = part_rows // part_cols if one_owner else 1
    count = 2 * groups
    pieces = jnp.split(panel, count, axis=0)
    reach = n_col
    while reach > 1:
        half = reach // 2
        pairs = [
            (r * n_col + c, r * n_col + c + half) for r in range(n_row) for c in range(0, n_col, reach)
        ]
        pieces = [spread(piece, pairs, me_col % reach == half) for piece in pieces]
        reach = half
    row_panel = jnp.concatenate(pieces, axis=0)
    if not one_owner:
        all_panel = lax.all_gather(row_panel, "row", axis=0, tiled=True)
        return row_panel, lax.dynamic_slice_in_dim(all_panel, me_col * part_cols, part_cols, 0)
    matching = []
    for k in range(2):
        piece = pieces[k]
        for g in range(1, groups):
            piece = jnp.where(me_col % groups == g, pieces[2 * g + k], piece)
        matching.append(piece)
    away = (me_row - me_col // groups + n_row) % n_row
    reach = n_row
    while reach > 1:
        half = reach // 2
        pairs = []
        for c in range(n_col):
            for i in range(0, n_row, reach):
                sender, receiver = (c // groups + i) % n_row, (c // groups + i + half) % n_row
                pairs.append((sender * n_col + c, receiver * n_col + c))
        matching = [spread(piece, pairs, away % reach == half) for piece in matching]
        reach = half
    return row_panel, jnp.concatenate(matching, axis=0)


def local(front_orig, child_updates, child_map, panel_inverse):
    n_row = lax.axis_size("row")
    n_col = lax.axis_size("col")
    me_row = lax.axis_index("row")
    me_col = lax.axis_index("col")
    rows_local, cols_local = child_updates.shape
    part_rows, part_cols = front_orig.shape
    senders = n_row // 2
    blocks_row = rows_local // B
    blocks_col = cols_local // B
    fine_count = max(n_row, n_col)
    prb = part_rows // B
    pcb = part_cols // B
    row_cap = max(1, blocks_row // fine_count) * (fine_count // n_row)
    col_cap = max(1, blocks_col // fine_count) * (fine_count // n_col)

    my_map = lax.dynamic_index_in_dim(child_map, me_row // senders, 0, keepdims=False)
    row_ids = lax.dynamic_slice_in_dim(child_map.reshape(-1), me_row * blocks_row, blocks_row)
    col_ids = lax.dynamic_slice_in_dim(my_map, me_col * blocks_col, blocks_col)
    row_src = source_of_slot(row_ids, prb, row_cap, n_row)
    col_src = source_of_slot(col_ids, pcb, col_cap, n_col)

    by_row = child_map.reshape(n_row, blocks_row)
    row_rank = rank_in_owner(by_row, by_row // prb).reshape(2, -1)
    sender = jnp.broadcast_to(
        jnp.arange(n_row, dtype=jnp.int32)[:, None], by_row.shape
    ).reshape(2, -1)
    mine = me_row * prb + jnp.arange(prb, dtype=jnp.int32)
    match = by_row.reshape(2, 1, -1) == mine[None, :, None]
    src = jnp.sum(jnp.where(match, sender[:, None, :], 0), axis=2)
    slot = jnp.sum(jnp.where(match, row_rank[:, None, :], 0), axis=2)
    has_row = jnp.sum(match, axis=2, dtype=jnp.int32)

    by_col = child_map.reshape(2, n_col, blocks_col)
    col_owner = by_col // pcb
    col_rank = rank_in_owner(by_col, col_owner)
    match = (col_owner == me_col)[:, :, None, :] & (
        col_rank[:, :, None, :] == jnp.arange(col_cap, dtype=jnp.int32)[None, None, :, None]
    )
    col_to = pcb + jnp.sum(
        jnp.where(match, (by_col - me_col * pcb - pcb)[:, :, None, :], 0), axis=3
    ).reshape(2, n_col * col_cap)

    head = min(PANEL_BLOCKS, col_cap)
    chunks = [(0, head)] + ([(head, col_cap - head)] if col_cap > head else [])
    incoming = []
    for first, width in chunks:
        outgoing = pack(
            child_updates, row_src, col_src, n_row, n_col, row_cap, col_cap, first, width
        ).reshape(n_row * n_col, row_cap * B, width * B)
        arrived = lax.all_to_all(outgoing, ("row", "col"), split_axis=0, concat_axis=0, tiled=True)
        incoming.append(arrived.reshape(n_row, n_col, row_cap * B, width * B))

    group = largest_group(prb, 2)
    panel_to = jnp.minimum(col_to, PANEL_BLOCKS)
    local_panel = gather_call(
        functools.partial(panel_kernel, group, chunks[:1], n_col, col_cap),
        (src, slot, has_row, panel_to), front_orig, (panel_inverse,),
        [pl.BlockSpec((PANEL, PANEL), lambda s, *_: (0, 0))],
        incoming[:1], chunks[:1], PANEL + B, group, PANEL, PANEL,
        2 * part_rows * PANEL * PANEL,
    )
    row_panel, col_panel = share_panel(local_panel, part_cols)
    strip = part_cols // largest_group(part_cols // PANEL, 5)
    schur = gather_call(
        functools.partial(schur_kernel, group, chunks, n_col, col_cap, strip),
        (src, slot, has_row, col_to), front_orig, (row_panel, col_panel),
        [
            pl.BlockSpec((group * B, PANEL), lambda s, *_: (s, 0)),
            pl.BlockSpec((part_cols, PANEL), lambda s, *_: (0, 0)),
        ],
        incoming, chunks, part_cols + B, group, part_cols, part_cols,
        2 * part_rows * part_cols * PANEL,
    )
    return (schur, row_panel)


def solution(mesh):
    in_specs = (P(("hyp", "row"), "col"), P(("hyp", "row"), "col"), P("hyp", None), P("hyp", None))
    out_specs = (P(("hyp", "row"), "col"), P(("hyp", "row"), None))
    return jax.shard_map(local, mesh=mesh, in_specs=in_specs, out_specs=out_specs, check_vma=False)
```

```python
import functools

import jax
import jax.numpy as jnp
from jax import lax
from jax.experimental import pallas as pl
from jax.experimental.pallas import tpu as pltpu
from jax.sharding import PartitionSpec as P

B = 128
PANEL = 256
PANEL_BLOCKS = PANEL // B
VMEM_LIMIT = 48 * 1024 * 1024


def largest_group(count, limit):
    return max(g for g in range(1, limit + 1) if count % g == 0)


def rank_in_owner(ids, owners):
    same = owners[..., :, None] == owners[..., None, :]
    smaller = ids[..., None, :] < ids[..., :, None]
    return jnp.sum(same & smaller, axis=-1, dtype=jnp.int32)


def source_of_slot(ids, owner_width, capacity, owners_count):
    owners = ids // owner_width
    slots = owners * capacity + rank_in_owner(ids, owners)
    match = slots[None, :] == jnp.arange(owners_count * capacity, dtype=jnp.int32)[:, None]
    return jnp.sum(jnp.where(match, jnp.arange(ids.shape[0], dtype=jnp.int32)[None, :], 0), axis=1)


def pack_kernel(group, n_col, col_cap, first, width, row_src, col_src, *refs):
    out = refs[group]
    for c in range(n_col):
        for b in range(width):
            src = pl.multiple_of(col_src[c * col_cap + first + b] * B, B)
            for g in range(group):
                out[0, c, g * B:(g + 1) * B, b * B:(b + 1) * B] = refs[g][:, pl.ds(src, B)]


def pack(child, row_src, col_src, n_row, n_col, row_cap, col_cap, first, width):
    group = largest_group(row_cap, 8)
    steps = row_cap // group
    cols = child.shape[1]

    def row_map(g, r, s, row_src, col_src):
        return (row_src[r * row_cap + s * group + g], 0)

    out_shape = (n_row, n_col, row_cap * B, width * B)
    size = n_row * n_col * row_cap * width * B * B
    return pl.pallas_call(
        functools.partial(pack_kernel, group, n_col, col_cap, first, width),
        grid_spec=pltpu.PrefetchScalarGridSpec(
            num_scalar_prefetch=2,
            grid=(n_row, steps),
            in_specs=[pl.BlockSpec((B, cols), functools.partial(row_map, g)) for g in range(group)],
            out_specs=pl.BlockSpec(
                (1, n_col, group * B, width * B), lambda r, s, row_src, col_src: (r, 0, s, 0)
            ),
        ),
        out_shape=jax.ShapeDtypeStruct(out_shape, jnp.bfloat16),
        compiler_params=pltpu.CompilerParams(vmem_limit_bytes=VMEM_LIMIT),
        cost_estimate=pl.CostEstimate(
            flops=0, bytes_accessed=2 * child.size + 2 * size, transcendentals=0
        ),
    )(row_src, col_src, *([child] * group))


def add_tiles(acc, group, chunks, n_col, col_cap, has_row, col_to, tiles):
    step = pl.program_id(0)
    for g in range(group):
        for k in range(2):
            @pl.when(has_row[k, step * group + g] > 0)
            def _():
                for h, (first, width) in enumerate(chunks):
                    ref = tiles[(g * 2 + k) * len(chunks) + h]
                    for t in range(n_col):
                        for b in range(width):
                            at = pl.multiple_of(col_to[k, t * col_cap + first + b] * B, B)
                            acc[g * B:(g + 1) * B, pl.ds(at, B)] += ref[
                                0, t, :, b * B:(b + 1) * B
                            ].astype(jnp.float32)


def panel_kernel(group, chunks, n_col, col_cap, src, slot, has_row, col_to, *refs):
    front_ref, inverse_ref = refs[:2]
    tiles, out, acc = refs[2:-2], refs[-2], refs[-1]
    acc[:, :PANEL] = front_ref[...].astype(jnp.float32)
    add_tiles(acc, group, chunks, n_col, col_cap, has_row, col_to, tiles)
    out[...] = jnp.dot(
        acc[:, :PANEL].astype(jnp.bfloat16), inverse_ref[...], preferred_element_type=jnp.float32
    ).astype(jnp.bfloat16)


def schur_kernel(group, chunks, n_col, col_cap, strip, src, slot, has_row, col_to, *refs):
    front_ref, row_ref, col_ref = refs[:3]
    tiles, out, acc = refs[3:-2], refs[-2], refs[-1]
    width = front_ref.shape[1]
    acc[:, :width] = front_ref[...].astype(jnp.float32)
    add_tiles(acc, group, chunks, n_col, col_cap, has_row, col_to, tiles)
    for at in range(0, width, strip):
        update = lax.dot_general(
            row_ref[...], col_ref[at:at + strip, :], (((1,), (1,)), ((), ())),
            preferred_element_type=jnp.float32,
        )
        front = acc[:, at:at + strip].astype(jnp.bfloat16).astype(jnp.float32)
        out[:, at:at + strip] = (front - update).astype(jnp.bfloat16)


def gather_call(body, tables, front, extra, extra_specs, incoming, chunks, acc_cols, group, out_cols,
                front_cols, flops):
    rows = front.shape[0]
    specs, arrays = [], []

    def tile_map(g, k, s, src, slot, has_row, col_to):
        return (src[k, s * group + g], 0, slot[k, s * group + g], 0)

    for g in range(group):
        for k in range(2):
            for array in incoming:
                n_col, width = array.shape[1], array.shape[3]
                specs.append(pl.BlockSpec((1, n_col, B, width), functools.partial(tile_map, g, k)))
                arrays.append(array)
    moved = rows * (front_cols + out_cols) * 2 + sum(2 * a.size for a in incoming)
    return pl.pallas_call(
        body,
        grid_spec=pltpu.PrefetchScalarGridSpec(
            num_scalar_prefetch=4,
            grid=(rows // (group * B),),
            in_specs=[pl.BlockSpec((group * B, front_cols), lambda s, *_: (s, 0))]
            + extra_specs + specs,
            out_specs=pl.BlockSpec((group * B, out_cols), lambda s, *_: (s, 0)),
            scratch_shapes=[pltpu.VMEM((group * B, acc_cols), jnp.float32)],
        ),
        out_shape=jax.ShapeDtypeStruct((rows, out_cols), jnp.bfloat16),
        compiler_params=pltpu.CompilerParams(vmem_limit_bytes=VMEM_LIMIT),
        cost_estimate=pl.CostEstimate(flops=flops, bytes_accessed=moved, transcendentals=0),
    )(*tables, front, *extra, *arrays)


def spread(value, pairs):
    return value + lax.ppermute(value, ("row", "col"), pairs)


def share_panel(panel, part_cols):
    n_row, n_col = lax.axis_size("row"), lax.axis_size("col")
    me_row, me_col = lax.axis_index("row"), lax.axis_index("col")
    part_rows = panel.shape[0]
    one_owner = part_rows % part_cols == 0
    groups = part_rows // part_cols if one_owner else 1
    count = 2 * groups
    held = jnp.where(me_col == 0, panel, jnp.zeros_like(panel))
    pieces = lax.optimization_barrier(tuple(jnp.split(held, count, axis=0)))
    reach = n_col
    while reach > 1:
        half = reach // 2
        pairs = [
            (r * n_col + c, r * n_col + c + half) for r in range(n_row) for c in range(0, n_col, reach)
        ]
        pieces = [spread(piece, pairs) for piece in pieces]
        reach = half
    row_panel = jnp.concatenate(pieces, axis=0)
    if not one_owner:
        all_panel = lax.all_gather(row_panel, "row", axis=0, tiled=True)
        return row_panel, lax.dynamic_slice_in_dim(all_panel, me_col * part_cols, part_cols, 0)
    matching = []
    for k in range(2):
        piece = pieces[k]
        for g in range(1, groups):
            piece = jnp.where(me_col % groups == g, pieces[2 * g + k], piece)
        owner = me_row == me_col // groups
        matching.append(jnp.where(owner, piece, jnp.zeros_like(piece)))
    reach = n_row
    while reach > 1:
        half = reach // 2
        pairs = []
        for c in range(n_col):
            for i in range(0, n_row, reach):
                sender, receiver = (c // groups + i) % n_row, (c // groups + i + half) % n_row
                pairs.append((sender * n_col + c, receiver * n_col + c))
        matching = [spread(piece, pairs) for piece in matching]
        reach = half
    return row_panel, jnp.concatenate(matching, axis=0)


def local(front_orig, child_updates, child_map, panel_inverse):
    n_row = lax.axis_size("row")
    n_col = lax.axis_size("col")
    me_row = lax.axis_index("row")
    me_col = lax.axis_index("col")
    rows_local, cols_local = child_updates.shape
    part_rows, part_cols = front_orig.shape
    senders = n_row // 2
    blocks_row = rows_local // B
    blocks_col = cols_local // B
    fine_count = max(n_row, n_col)
    prb = part_rows // B
    pcb = part_cols // B
    row_cap = max(1, blocks_row // fine_count) * (fine_count // n_row)
    col_cap = max(1, blocks_col // fine_count) * (fine_count // n_col)

    my_map = lax.dynamic_index_in_dim(child_map, me_row // senders, 0, keepdims=False)
    row_ids = lax.dynamic_slice_in_dim(child_map.reshape(-1), me_row * blocks_row, blocks_row)
    col_ids = lax.dynamic_slice_in_dim(my_map, me_col * blocks_col, blocks_col)
    row_src = source_of_slot(row_ids, prb, row_cap, n_row)
    col_src = source_of_slot(col_ids, pcb, col_cap, n_col)

    by_row = child_map.reshape(n_row, blocks_row)
    row_rank = rank_in_owner(by_row, by_row // prb).reshape(2, -1)
    sender = jnp.broadcast_to(
        jnp.arange(n_row, dtype=jnp.int32)[:, None], by_row.shape
    ).reshape(2, -1)
    mine = me_row * prb + jnp.arange(prb, dtype=jnp.int32)
    match = by_row.reshape(2, 1, -1) == mine[None, :, None]
    src = jnp.sum(jnp.where(match, sender[:, None, :], 0), axis=2)
    slot = jnp.sum(jnp.where(match, row_rank[:, None, :], 0), axis=2)
    has_row = jnp.sum(match, axis=2, dtype=jnp.int32)

    by_col = child_map.reshape(2, n_col, blocks_col)
    col_owner = by_col // pcb
    col_rank = rank_in_owner(by_col, col_owner)
    match = (col_owner == me_col)[:, :, None, :] & (
        col_rank[:, :, None, :] == jnp.arange(col_cap, dtype=jnp.int32)[None, None, :, None]
    )
    col_to = pcb + jnp.sum(
        jnp.where(match, (by_col - me_col * pcb - pcb)[:, :, None, :], 0), axis=3
    ).reshape(2, n_col * col_cap)

    head = min(PANEL_BLOCKS, col_cap)
    chunks = [(0, head)] + ([(head, col_cap - head)] if col_cap > head else [])
    incoming = []
    for first, width in chunks:
        outgoing = pack(
            child_updates, row_src, col_src, n_row, n_col, row_cap, col_cap, first, width
        ).reshape(n_row * n_col, row_cap * B, width * B)
        arrived = lax.all_to_all(outgoing, ("row", "col"), split_axis=0, concat_axis=0, tiled=True)
        incoming.append(arrived.reshape(n_row, n_col, row_cap * B, width * B))

    group = largest_group(prb, 4)
    panel_to = jnp.minimum(col_to, PANEL_BLOCKS)
    local_panel = gather_call(
        functools.partial(panel_kernel, group, chunks[:1], n_col, col_cap),
        (src, slot, has_row, panel_to), front_orig, (panel_inverse,),
        [pl.BlockSpec((PANEL, PANEL), lambda s, *_: (0, 0))],
        incoming[:1], chunks[:1], PANEL + B, group, PANEL, PANEL,
        2 * part_rows * PANEL * PANEL,
    )
    row_panel, col_panel = share_panel(local_panel, part_cols)
    strip = part_cols // largest_group(part_cols // PANEL, 5)
    schur = gather_call(
        functools.partial(schur_kernel, group, chunks, n_col, col_cap, strip),
        (src, slot, has_row, col_to), front_orig, (row_panel, col_panel),
        [
            pl.BlockSpec((group * B, PANEL), lambda s, *_: (s, 0)),
            pl.BlockSpec((part_cols, PANEL), lambda s, *_: (0, 0)),
        ],
        incoming, chunks, part_cols + B, group, part_cols, part_cols,
        2 * part_rows * part_cols * PANEL,
    )
    return (schur, row_panel)


def solution(mesh):
    in_specs = (P(("hyp", "row"), "col"), P(("hyp", "row"), "col"), P("hyp", None), P("hyp", None))
    out_specs = (P(("hyp", "row"), "col"), P(("hyp", "row"), None))
    return jax.shard_map(local, mesh=mesh, in_specs=in_specs, out_specs=out_specs, check_vma=False)
```
